32 devices in a mesh: groups: 2 (over y), tensor: 4 (over z), dp: 4 (over x, core).
Axes of the slice: x: 2, y: 2, z: 4, core: 2. Of those that a mesh axis runs over, the one named last changes fastest.
Arguments:
- tokens_in: bfloat16 [1024, 4096], P(('groups', 'dp'), 'tensor'), parts along dimension 0, may hold values from -6 to 6
- hidden_grad: bfloat16 [1024, 112, 128], P(('groups', 'dp'), 'tensor'), parts along dimension 0, may hold values from -6 to 6
- gate_blocks: bfloat16 [112, 16, 128, 128], P('tensor'), may hold values from -0.125 to 0.125
- up_blocks: bfloat16 [112, 16, 128, 128], P('tensor'), may hold values from -0.125 to 0.125
- gate_rows: int32 [112, 16], replicated, may hold values from 0 to 31, as said below
- up_rows: int32 [112, 16], replicated, may hold values from 0 to 31, as said below
- column_of_slot: int32 [112], P('tensor'), may hold values from 0 to 111, as said below
Outputs:
- tokens_grad: bfloat16 [1024, 4096], P(('groups', 'dp'), 'tensor'), parts along dimension 0
- gate_grad: bfloat16 [112, 32, 128, 128], P('tensor', ('groups', 'dp')), parts along dimension 1
- up_grad: bfloat16 [112, 32, 128, 128], P('tensor', ('groups', 'dp')), parts along dimension 1
The draws below stay inside these ranges and needn't reach their ends.
There are 2 independent parts, one for each index of `groups`. The reference program is written for one: setup_inputs(seed, part) draws one part's arguments, and reference() takes and returns one part's arrays. A program takes and returns all parts, laid end to end along the dimension named above; an argument that names none is the same for every part. Nothing has to cross between parts.
Inputs may be any that keep to these rules, and one draw needn't show every extreme that they name: `gate_rows`: each row holds 16 distinct row blocks in rising order. `up_rows`: each row holds 16 distinct row blocks in rising order. `column_of_slot`: every column block 0 to 111 stands in exactly one slot; the other slots hold 112; slot s lies on tensor index s // 28.
All inputs are finite; a program needn't handle non-finite values.
Results may differ from the reference program's by a relative error of at most 0.009.
Values may be sent and summed in bfloat16 or wider, within the bound.
A program may use at most 384 MiB of HBM per device.

```python
import jax
import jax.numpy as jnp
from jax import lax

D = 4096
BLK = 128
TOK_DEV = 128
DB = 32
FB = 112
NNZ = 16
CAP = 28
SLOTS = 112
TOKENS = 512
N_TENSOR = 4
N_DP = 4


def pick_rows(key):
    row_keys = jax.random.split(key, FB)
    shuffled = jax.vmap(lambda one_key: jax.random.permutation(one_key, DB))(row_keys)
    return jnp.sort(shuffled[:, :NNZ], axis=1).astype(jnp.int32)


def draw_gate_rows(key, part):
    key = jax.random.fold_in(key, 1)
    return pick_rows(key)


def draw_up_rows(key, part):
    key = jax.random.fold_in(key, 2)
    return pick_rows(key)


def draw_column_of_slot(key, part):
    key = jax.random.fold_in(key, 3)
    shuffled = jax.random.permutation(key, SLOTS).astype(jnp.int32)
    return jnp.where(shuffled < FB, shuffled, FB).astype(jnp.int32)


def block_scale(key, dims, pieces, low, largest):
    def one(dim, blocks):
        heights = jax.random.uniform(jax.random.fold_in(jax.random.fold_in(key, 6), dim), (blocks,), jnp.float32, low / len(pieces), largest / len(pieces))
        return jnp.repeat(jnp.exp(heights), dims[dim] // blocks).reshape((-1,) + (1,) * (len(dims) - dim - 1))

    level = one(*pieces[0])
    for cut in pieces[1:]:
        level = level * one(*cut)
    return level


def centred(own_key, shape, spread, limit, pieces=(), kind=jnp.bfloat16):
    values = jax.random.normal(own_key, shape, jnp.float32) * spread
    if len(pieces) > 0:
        values = block_scale(own_key, shape, pieces, -0.22, 0.18) * values
    return jnp.clip(values, min=-limit, max=limit).astype(kind)


def setup_inputs(seed: int = 0, part: int = 0) -> dict:
    key_list = jax.random.split(jax.random.key(seed), 8)
    part_splits = jax.random.split(jax.random.fold_in(key_list[7], part), 8)
    return {
        "tokens_in": centred(part_splits[0], (TOKENS, D), 1.0, 6.0, ((0, 4), (1, 4))),
        "hidden_grad": centred(part_splits[1], (TOKENS, SLOTS, BLK), 1.0, 6.0, ((0, 4), (1, 4))),
        "gate_blocks": centred(key_list[2], (SLOTS, NNZ, BLK, BLK), (NNZ * BLK) ** -0.5, 0.125, ((0, 4),)),
        "up_blocks": centred(key_list[3], (SLOTS, NNZ, BLK, BLK), (NNZ * BLK) ** -0.5, 0.125, ((0, 4),)),
        "gate_rows": draw_gate_rows(jax.random.fold_in(key_list[7], 71), part),
        "up_rows": draw_up_rows(jax.random.fold_in(key_list[7], 71), part),
        "column_of_slot": draw_column_of_slot(jax.random.fold_in(key_list[7], 71), part),
    }


def cotangents(gate_value, up_value, hidden_cot):
    sigmoid_gate = jax.nn.sigmoid(gate_value)
    gate_cot = hidden_cot * up_value * sigmoid_gate * (1.0 + gate_value * (1.0 - sigmoid_gate))
    up_cot = hidden_cot * gate_value * sigmoid_gate
    return gate_cot.astype(jnp.bfloat16), up_cot.astype(jnp.bfloat16)


def reference(tokens_in, hidden_grad, gate_blocks, up_blocks, gate_rows, up_rows, column_of_slot):
    safe_column = jnp.minimum(column_of_slot, FB - 1)
    in_use = (column_of_slot < FB).astype(jnp.float32).reshape(N_TENSOR, CAP)
    rows_gate = jnp.take(gate_rows, safe_column, axis=0).astype(jnp.int32).reshape(N_TENSOR, CAP * NNZ)
    rows_up = jnp.take(up_rows, safe_column, axis=0).astype(jnp.int32).reshape(N_TENSOR, CAP * NNZ)
    weights_gate = gate_blocks.reshape(N_TENSOR, CAP, NNZ, BLK, BLK)
    weights_up = up_blocks.reshape(N_TENSOR, CAP, NNZ, BLK, BLK)

    def replica(totals, inputs_one):
        x_tokens, hidden_one = inputs_one
        token_blocks = x_tokens.reshape(TOK_DEV, DB, BLK).astype(jnp.float32)
        hidden_owner = hidden_one.reshape(TOK_DEV, N_TENSOR, CAP, BLK).transpose(1, 0, 2, 3)

        def per_owner(owner_inputs):
            row_gate, row_up, w_gate, w_up, keep_mask, hidden_cot = owner_inputs
            picked_gate = jnp.take(token_blocks, row_gate, axis=1).reshape(TOK_DEV, CAP, NNZ, BLK)
            picked_up = jnp.take(token_blocks, row_up, axis=1).reshape(TOK_DEV, CAP, NNZ, BLK)
            gate_value = jnp.einsum('tsnb,snbc->tsc', picked_gate, w_gate.astype(jnp.float32))
            up_value = jnp.einsum('tsnb,snbc->tsc', picked_up, w_up.astype(jnp.float32))
            masked = hidden_cot.astype(jnp.float32) * keep_mask[None, :, None]
            gate_cot, up_cot = cotangents(gate_value, up_value, masked)
            back_gate = jnp.einsum('tsc,snbc->tsnb', gate_cot.astype(jnp.float32), w_gate.astype(jnp.float32))
            back_up = jnp.einsum('tsc,snbc->tsnb', up_cot.astype(jnp.float32), w_up.astype(jnp.float32))
            partial_value = jnp.zeros((TOK_DEV, DB, BLK), jnp.float32)
            partial_value = partial_value.at[:, row_gate].add(back_gate.reshape(TOK_DEV, CAP * NNZ, BLK))
            partial_value = partial_value.at[:, row_up].add(back_up.reshape(TOK_DEV, CAP * NNZ, BLK))
            grad_gate = jnp.einsum('tsnb,tsc->snbc', picked_gate, gate_cot.astype(jnp.float32))
            grad_up = jnp.einsum('tsnb,tsc->snbc', picked_up, up_cot.astype(jnp.float32))
            return (partial_value.reshape(TOK_DEV, D).astype(jnp.bfloat16), grad_gate.astype(jnp.bfloat16), grad_up.astype(jnp.bfloat16))

        partials, grads_gate, grads_up = lax.map(per_owner, (rows_gate, rows_up, weights_gate, weights_up, in_use, hidden_owner))
        x_grad = jnp.sum(partials.astype(jnp.float32), axis=0).astype(jnp.bfloat16)
        return (totals[0] + grads_gate.astype(jnp.float32), totals[1] + grads_up.astype(jnp.float32)), x_grad

    zeros_grad = jnp.zeros((N_TENSOR, CAP, NNZ, BLK, BLK), jnp.float32)
    sums, x_grads = lax.scan(replica, (zeros_grad, zeros_grad), (tokens_in.reshape(N_DP, TOK_DEV, D), hidden_grad.reshape(N_DP, TOK_DEV, SLOTS, BLK)))
    tokens_grad = x_grads.reshape(TOKENS, D)
    gate_grad = sums[0].reshape(SLOTS, NNZ, BLK, BLK).astype(jnp.bfloat16)
    up_grad = sums[1].reshape(SLOTS, NNZ, BLK, BLK).astype(jnp.bfloat16)
    return (tokens_grad, gate_grad, up_grad)
```

```python
import functools

import jax
import jax.numpy as jnp
from jax import lax
from jax.experimental import pallas as pl
from jax.experimental.pallas import tpu as pltpu
from jax.sharding import PartitionSpec as P

VMEM_LIMIT = 48 * 1024 * 1024
CHUNKS = 2


def nt(a, b):
    return lax.dot_general(a, b, (((1,), (1,)), ((), ())), preferred_element_type=jnp.float32)


def slot_kernel(first, nonzero, rows_gate, rows_up, x_ref, hid_ref, wg_ref, wu_ref, start_ref, cot_ref, acc_ref):
    step = pl.program_id(0)
    slot = first + step

    @pl.when(step == 0)
    def _():
        acc_ref[...] = start_ref[...]

    block = wg_ref.shape[-1]
    depth = nonzero * block
    picked_gate = jnp.concatenate([x_ref[rows_gate[slot, k]] for k in range(nonzero)], axis=1)
    gate = jnp.dot(picked_gate, wg_ref[0].reshape(depth, block), preferred_element_type=jnp.float32)
    picked_up = jnp.concatenate([x_ref[rows_up[slot, k]] for k in range(nonzero)], axis=1)
    up = jnp.dot(picked_up, wu_ref[0].reshape(depth, block), preferred_element_type=jnp.float32)
    hid = hid_ref[0].astype(jnp.float32)
    p = jax.nn.sigmoid(gate)
    gate_cot = (hid * up * p * (1.0 + gate * (1.0 - p))).astype(jnp.bfloat16)
    up_cot = (hid * gate * p).astype(jnp.bfloat16)
    cot_ref[0, 0] = gate_cot
    cot_ref[0, 1] = up_cot
    for rows, cot, w_ref in ((rows_gate, gate_cot, wg_ref), (rows_up, up_cot, wu_ref)):
        for k in range(0, nonzero, 2):
            pair = nt(cot, w_ref[0, k : k + 2].reshape(2 * block, block))
            acc_ref[rows[slot, k]] += pair[:, :block]
            acc_ref[rows[slot, k + 1]] += pair[:, block:]


def slots_call(first, count, rows_gate, rows_up, x_blocks, hid, wg, wu, start):
    row_blocks, tokens, block = x_blocks.shape
    nonzero = wg.shape[1]
    whole = pl.BlockSpec(x_blocks.shape, lambda i, a, b: (0, 0, 0))
    weight = pl.BlockSpec((1, nonzero, block, block), lambda i, a, b: (first + i, 0, 0, 0))
    flops = count * nonzero * 2 * 2 * 2 * tokens * block * block
    return pl.pallas_call(
        functools.partial(slot_kernel, first, nonzero),
        grid_spec=pltpu.PrefetchScalarGridSpec(
            num_scalar_prefetch=2,
            grid=(count,),
            in_specs=[
                whole,
                pl.BlockSpec((1, tokens, block), lambda i, a, b: (first + i, 0, 0)),
                weight,
                weight,
                whole,
            ],
            out_specs=[
                pl.BlockSpec((1, 2, tokens, block), lambda i, a, b: (i, 0, 0, 0)),
                whole,
            ],
        ),
        out_shape=[
            jax.ShapeDtypeStruct((count, 2, tokens, block), jnp.bfloat16),
            jax.ShapeDtypeStruct(x_blocks.shape, jnp.float32),
        ],
        compiler_params=pltpu.CompilerParams(
            dimension_semantics=("arbitrary",), vmem_limit_bytes=VMEM_LIMIT
        ),
        cost_estimate=pl.CostEstimate(
            flops=flops, bytes_accessed=count * nonzero * 4 * block * block, transcendentals=0
        ),
    )(rows_gate, rows_up, x_blocks, hid, wg, wu, start)


def grad_kernel(first, replicas, rows_gate, rows_up, xt_ref, cot_ref, *rest):
    gg_ref, gu_ref = rest[-2:]
    slot = first + pl.program_id(0)
    own = gg_ref.shape[1]
    per = xt_ref.shape[1]
    block = gg_ref.shape[-1]
    for which, (rows, out_ref) in enumerate(((rows_gate, gg_ref), (rows_up, gu_ref))):
        cot = cot_ref[:, 0, which].reshape(-1, block)
        for k in range(own):
            row = rows[slot, k]
            owner = lax.div(row, per)
            inner = row - owner * per
            lhs = jnp.concatenate(
                [xt_ref[owner * replicas + r, inner] for r in range(replicas)], axis=1
            )
            out_ref[0, k] = jnp.dot(lhs, cot, preferred_element_type=jnp.float32).astype(jnp.bfloat16)


def grads_call(first, count, slot_count, replicas, rows_gate, rows_up, xt, cots, before):
    own = rows_gate.shape[1]
    tokens, block = cots.shape[-2:]
    out = jax.ShapeDtypeStruct((slot_count, own, block, block), jnp.bfloat16)
    out_spec = pl.BlockSpec((1, own, block, block), lambda i, a, b: (first + i, 0, 0, 0))
    extra = () if before is None else before
    return pl.pallas_call(
        functools.partial(grad_kernel, first, replicas),
        grid_spec=pltpu.PrefetchScalarGridSpec(
            num_scalar_prefetch=2,
            grid=(count,),
            in_specs=[
                pl.BlockSpec(xt.shape, lambda i, a, b: (0, 0, 0, 0)),
                pl.BlockSpec((replicas, 1, 2, tokens, block), lambda i, a, b: (0, i, 0, 0, 0)),
            ]
            + [pl.BlockSpec(memory_space=pl.ANY)] * len(extra),
            out_specs=[out_spec, out_spec],
        ),
        out_shape=[out, out],
        input_output_aliases={} if before is None else {4: 0, 5: 1},
        compiler_params=pltpu.CompilerParams(
            dimension_semantics=("arbitrary",), vmem_limit_bytes=VMEM_LIMIT
        ),
        cost_estimate=pl.CostEstimate(
            flops=count * own * 2 * 2 * replicas * tokens * block * block,
            bytes_accessed=count * own * 4 * block * block,
            transcendentals=0,
        ),
    )(rows_gate, rows_up, xt, cots, *extra)


def body(tokens_in, hidden_grad, gate_blocks, up_blocks, gate_rows, up_rows, column_of_slot):
    tokens, local_width = tokens_in.shape
    slot_count, nonzero, block = gate_blocks.shape[:3]
    column_count = gate_rows.shape[0]
    owners = lax.axis_size("tensor")
    replicas = lax.axis_size("dp")
    per = local_width // block
    own = nonzero // replicas
    column_hot = (
        column_of_slot[:, None] == jnp.arange(column_count, dtype=jnp.int32)[None, :]
    ).astype(jnp.int32)
    rows_gate = jnp.sum(column_hot[:, :, None] * gate_rows[None, :, :], axis=1)
    rows_up = jnp.sum(column_hot[:, :, None] * up_rows[None, :, :], axis=1)
    in_use = (column_of_slot < column_count).astype(jnp.bfloat16)

    x_local = tokens_in.reshape(tokens, per, block).transpose(1, 0, 2)
    x_blocks = lax.all_gather(x_local, "tensor", axis=0, tiled=True)
    hid = (hidden_grad * in_use[None, :, None]).transpose(1, 0, 2)
    xt_local = tokens_in.T.reshape(per, block, tokens)
    xt = lax.all_gather(xt_local, ("tensor", "dp"), axis=0, tiled=False)

    index = lax.axis_index("dp")
    own_gate = lax.dynamic_slice_in_dim(rows_gate, index * own, own, axis=1)
    own_up = lax.dynamic_slice_in_dim(rows_up, index * own, own, axis=1)

    chunks = CHUNKS if slot_count % CHUNKS == 0 else 1
    count = slot_count // chunks
    total = jnp.zeros(x_blocks.shape, jnp.float32)
    gathered = []
    for c in range(chunks):
        cots, total = slots_call(
            c * count, count, rows_gate, rows_up, x_blocks, hid, gate_blocks, up_blocks, total
        )
        gathered.append(lax.all_gather(cots, "dp", axis=0, tiled=False))
    arrived = lax.all_to_all(
        total.astype(jnp.bfloat16).reshape(owners, per, tokens, block),
        "tensor",
        split_axis=0,
        concat_axis=0,
        tiled=True,
    )
    tokens_grad = (
        jnp.sum(arrived.astype(jnp.float32), axis=0)
        .astype(jnp.bfloat16)
        .transpose(1, 0, 2)
        .reshape(tokens, local_width)
    )
    grads = None
    for c in range(chunks):
        grads = grads_call(
            c * count, count, slot_count, replicas, own_gate, own_up, xt, gathered[c], grads
        )
    return (tokens_grad, grads[0], grads[1])


def solution(mesh):
    placed = (
        P(("groups", "dp"), "tensor"),
        P(("groups", "dp"), "tensor", None),
        P("tensor", None, None, None),
        P("tensor", None, None, None),
        P(),
        P(),
        P("tensor"),
    )
    return jax.shard_map(
        body,
        mesh=mesh,
        in_specs=placed,
        out_specs=(
            P(("groups", "dp"), "tensor"),
            P("tensor", ("groups", "dp"), None, None),
            P("tensor", ("groups", "dp"), None, None),
        ),
        check_vma=False,
    )
```

```python
import functools

import jax
import jax.numpy as jnp
from jax import lax
from jax.experimental import pallas as pl
from jax.experimental.pallas import tpu as pltpu
from jax.sharding import PartitionSpec as P

VMEM_LIMIT = 48 * 1024 * 1024
MESH = pl.DeviceIdType.MESH


def gather_kernel(owners, x_ref, hid_ref, xall_ref, hall_ref, send_x, recv_x, send_h, recv_h,
                  send_z, recv_z, send_sx, recv_sx, send_sh, recv_sh, local_sem):
    me = lax.axis_index("tensor")
    rep = lax.axis_index("dp")
    sib = rep + 1 - 2 * lax.rem(rep, 2)
    far = lax.rem(rep + 2, 4)
    slots = hid_ref.shape[0]
    half = slots // 2
    has_left, has_right = me > 0, me < owners - 1

    barrier = pltpu.get_barrier_semaphore()
    pl.semaphore_signal(barrier, inc=1, device_id={"dp": sib}, device_id_type=MESH)
    pl.semaphore_signal(barrier, inc=1, device_id={"dp": far}, device_id_type=MESH)

    @pl.when(has_left)
    def _():
        pl.semaphore_signal(barrier, inc=1, device_id={"tensor": me - 1}, device_id_type=MESH)

    @pl.when(has_right)
    def _():
        pl.semaphore_signal(barrier, inc=1, device_id={"tensor": me + 1}, device_id_type=MESH)

    inner = jnp.where(has_left, 1, 0) + jnp.where(has_right, 1, 0)
    pl.semaphore_wait(barrier, 2 + inner)

    def remote(src, dst, send, recv, where):
        return pltpu.make_async_remote_copy(
            src_ref=src, dst_ref=dst, send_sem=send, recv_sem=recv,
            device_id=where, device_id_type=MESH,
        )

    home = (rep, far)
    from_sib = (sib, lax.rem(sib + 2, 4))

    def far_x(d):
        return remote(x_ref, xall_ref.at[me, d], send_x, recv_x, {"dp": far})

    def far_h(d, piece):
        span = pl.ds(piece * half, half)
        return remote(hid_ref.at[span], hall_ref.at[d, span], send_h.at[piece], recv_h.at[piece], {"dp": far})

    def sib_x(cls, z, owner):
        src = x_ref if (cls == 0 and z is me) else xall_ref.at[z, owner[cls]]
        return remote(src, xall_ref.at[z, owner[cls]], send_sx.at[cls, z], recv_sx.at[cls, z], {"dp": sib})

    def sib_h(cls, piece, owner):
        span = pl.ds(piece * half, half)
        src = hid_ref.at[span] if cls == 0 else hall_ref.at[owner[cls], span]
        return remote(src, hall_ref.at[owner[cls], span], send_sh.at[cls, piece], recv_sh.at[cls, piece], {"dp": sib})

    def along(way, cls, hop, z, to):
        src = x_ref if (cls == 0 and hop == 1) else xall_ref.at[z, home[cls]]
        return remote(src, xall_ref.at[z, home[cls]], send_z.at[way, cls, hop - 1], recv_z.at[way, cls, hop - 1], {"tensor": to})

    def out(way, cls, hop, act):
        step = 1 - 2 * way
        z = me - step * (hop - 1)
        to = me + step
        ok = jnp.logical_and(jnp.logical_and(to >= 0, to < owners), jnp.logical_and(z >= 0, z < owners))

        @pl.when(ok)
        def _():
            act(along(way, cls, hop, jnp.clip(z, 0, owners - 1), jnp.clip(to, 0, owners - 1)))

    def arrive(way, cls, hop):
        step = 1 - 2 * way
        z = me - step * hop

        @pl.when(jnp.logical_and(z >= 0, z < owners))
        def _():
            zc = jnp.clip(z, 0, owners - 1)
            frm = jnp.clip(me - step, 0, owners - 1)
            along(way, cls, hop, zc, frm).wait_recv()
            sib_x(cls, zc, home).start()

    own_x = pltpu.make_async_copy(x_ref, xall_ref.at[me, rep], local_sem.at[0])
    own_h = pltpu.make_async_copy(hid_ref, hall_ref.at[rep], local_sem.at[1])

    far_x(rep).start()
    for way in range(2):
        out(way, 0, 1, lambda c: c.start())
    sib_x(0, me, home).start()
    for piece in range(2):
        far_h(rep, piece).start()
    for piece in range(2):
        sib_h(0, piece, home).start()
    own_x.start()
    own_h.start()
    far_x(far).wait_recv()
    for way in range(2):
        out(way, 1, 1, lambda c: c.start())
    sib_x(1, me, home).start()
    for hop in range(1, owners):
        for cls in range(2):
            for way in range(2):
                arrive(way, cls, hop)
                if hop + 1 < owners:
                    out(way, cls, hop + 1, lambda c: c.start())
        if hop == 2 or owners == 2:
            for piece in range(2):
                far_h(far, piece).wait_recv()
                sib_h(1, piece, home).start()

    own_x.wait()
    own_h.wait()
    far_x(rep).wait_send()
    for piece in range(2):
        far_h(rep, piece).wait_send()
    for hop in range(1, owners):
        for cls in range(2):
            for way in range(2):
                out(way, cls, hop, lambda c: c.wait_send())
    for cls in range(2):
        for piece in range(2):
            sib_h(cls, piece, home).wait_send()
            sib_h(cls, piece, from_sib).wait_recv()
        for z in range(owners):
            sib_x(cls, z, home).wait_send()
            sib_x(cls, z, from_sib).wait_recv()


def gather_all(x_local, hid):
    owners = lax.axis_size("tensor")
    replicas = lax.axis_size("dp")
    if replicas != 4 or owners < 2 or owners > 8 or hid.shape[0] % 2:
        x_all = lax.all_gather(lax.all_gather(x_local, "dp", axis=0), "tensor", axis=0)
        return x_all, lax.all_gather(hid, "dp", axis=0)
    dma = pltpu.SemaphoreType.DMA
    hops = owners - 1
    return pl.pallas_call(
        functools.partial(gather_kernel, owners),
        in_specs=[pl.BlockSpec(memory_space=pl.ANY)] * 2,
        out_specs=[pl.BlockSpec(memory_space=pl.ANY)] * 2,
        out_shape=[
            jax.ShapeDtypeStruct((owners, replicas) + x_local.shape, x_local.dtype),
            jax.ShapeDtypeStruct((replicas,) + hid.shape, hid.dtype),
        ],
        scratch_shapes=[
            dma, dma, dma((2,)), dma((2,)),
            dma((2, 2, hops)), dma((2, 2, hops)),
            dma((2, owners)), dma((2, owners)),
            dma((2, 2)), dma((2, 2)), dma((2,)),
        ],
        compiler_params=pltpu.CompilerParams(collective_id=0, has_side_effects=True),
    )(x_local, hid)


def slot_kernel(nonzero, rows_gate, rows_up, where, x_ref, hid_ref, wg_ref, wu_ref, cot_ref, out_ref, acc_ref):
    slot = pl.program_id(0)

    @pl.when(slot == 0)
    def _():
        acc_ref[...] = jnp.zeros_like(acc_ref)

    per = x_ref.shape[2]
    tokens = x_ref.shape[3]
    block = wg_ref.shape[-1]
    depth = nonzero * block
    rep = where[0]

    def product(rows, w_ref):
        parts = []
        for k in range(nonzero):
            row = rows[slot, k]
            owner = lax.div(row, per)
            parts.append(x_ref[owner, :, row - owner * per].reshape(-1, block))
        return jnp.dot(
            jnp.concatenate(parts, axis=1), w_ref[0].reshape(depth, block),
            preferred_element_type=jnp.float32,
        )

    gate = product(rows_gate, wg_ref)
    up = product(rows_up, wu_ref)
    hid = hid_ref[:, 0].reshape(-1, block).astype(jnp.float32)
    p = jax.nn.sigmoid(gate)
    gate_cot = (hid * up * p * (1.0 + gate * (1.0 - p))).astype(jnp.bfloat16)
    up_cot = (hid * gate * p).astype(jnp.bfloat16)
    cot_ref[0, 0] = gate_cot
    cot_ref[0, 1] = up_cot
    mine = pl.ds(pl.multiple_of(rep * tokens, tokens), tokens)
    for which, (rows, w_ref) in enumerate(((rows_gate, wg_ref), (rows_up, wu_ref))):
        cot = cot_ref[0, which, mine, :].T
        back = jnp.dot(w_ref[0].reshape(depth, block), cot, preferred_element_type=jnp.float32)
        for k in range(nonzero):
            acc_ref[rows[slot, k]] += back[k * block : (k + 1) * block]

    @pl.when(slot == pl.num_programs(0) - 1)
    def _():
        for r in range(acc_ref.shape[0]):
            out_ref[r] = acc_ref[r].T.astype(jnp.bfloat16)


def slots_call(rows_gate, rows_up, where, x_all, hid_all, wg, wu):
    owners, replicas, per, tokens, block = x_all.shape
    slot_count, nonzero = wg.shape[:2]
    row_blocks = owners * per
    weight = pl.BlockSpec((1, nonzero, block, block), lambda i, a, b, c: (i, 0, 0, 0))
    return pl.pallas_call(
        functools.partial(slot_kernel, nonzero),
        grid_spec=pltpu.PrefetchScalarGridSpec(
            num_scalar_prefetch=3,
            grid=(slot_count,),
            in_specs=[
                pl.BlockSpec(x_all.shape, lambda i, a, b, c: (0, 0, 0, 0, 0)),
                pl.BlockSpec((replicas, 1, tokens, block), lambda i, a, b, c: (0, i, 0, 0)),
                weight,
                weight,
            ],
            out_specs=[
                pl.BlockSpec((1, 2, replicas * tokens, block), lambda i, a, b, c: (i, 0, 0, 0)),
                pl.BlockSpec((row_blocks, tokens, block), lambda i, a, b, c: (0, 0, 0)),
            ],
            scratch_shapes=[pltpu.VMEM((row_blocks, block, tokens), jnp.float32)],
        ),
        out_shape=[
            jax.ShapeDtypeStruct((slot_count, 2, replicas * tokens, block), jnp.bfloat16),
            jax.ShapeDtypeStruct((row_blocks, tokens, block), jnp.bfloat16),
        ],
        compiler_params=pltpu.CompilerParams(
            dimension_semantics=("arbitrary",), vmem_limit_bytes=VMEM_LIMIT
        ),
        cost_estimate=pl.CostEstimate(
            flops=slot_count * nonzero * 2 * 5 * 2 * tokens * block * block,
            bytes_accessed=slot_count * nonzero * 4 * block * block,
            transcendentals=0,
        ),
    )(rows_gate, rows_up, where, x_all, hid_all, wg, wu)


def grad_kernel(rows_gate, rows_up, x_ref, cot_ref, gg_ref, gu_ref, xt_ref):
    slot = pl.program_id(0)
    owners, _, per, _, block = x_ref.shape
    own = gg_ref.shape[1]

    @pl.when(slot == 0)
    def _():
        for t in range(owners):
            for i in range(per):
                xt_ref[t * per + i] = x_ref[t, :, i].reshape(-1, block).T

    for which, (rows, out_ref) in enumerate(((rows_gate, gg_ref), (rows_up, gu_ref))):
        lhs = jnp.concatenate([xt_ref[rows[slot, k]] for k in range(own)], axis=0)
        both = jnp.dot(lhs, cot_ref[0, which], preferred_element_type=jnp.float32)
        out_ref[0] = both.reshape(own, block, block).astype(jnp.bfloat16)


def grads_call(rows_gate, rows_up, x_all, cots):
    own = rows_gate.shape[1]
    owners, replicas, per, tokens, block = x_all.shape
    slot_count = cots.shape[0]
    out = jax.ShapeDtypeStruct((slot_count, own, block, block), jnp.bfloat16)
    out_spec = pl.BlockSpec((1, own, block, block), lambda i, a, b: (i, 0, 0, 0))
    return pl.pallas_call(
        grad_kernel,
        grid_spec=pltpu.PrefetchScalarGridSpec(
            num_scalar_prefetch=2,
            grid=(slot_count,),
            in_specs=[
                pl.BlockSpec(x_all.shape, lambda i, a, b: (0, 0, 0, 0, 0)),
                pl.BlockSpec((1, 2, replicas * tokens, block), lambda i, a, b: (i, 0, 0, 0)),
            ],
            out_specs=[out_spec, out_spec],
            scratch_shapes=[pltpu.VMEM((owners * per, block, replicas * tokens), jnp.bfloat16)],
        ),
        out_shape=[out, out],
        compiler_params=pltpu.CompilerParams(
            dimension_semantics=("arbitrary",), vmem_limit_bytes=VMEM_LIMIT
        ),
        cost_estimate=pl.CostEstimate(
            flops=slot_count * own * 2 * 2 * replicas * tokens * block * block,
            bytes_accessed=slot_count * own * 4 * block * block,
            transcendentals=0,
        ),
    )(rows_gate, rows_up, x_all, cots)


def body(tokens_in, hidden_grad, gate_blocks, up_blocks, gate_rows, up_rows, column_of_slot):
    tokens, local_width = tokens_in.shape
    slot_count, nonzero, block = gate_blocks.shape[:3]
    column_count = gate_rows.shape[0]
    owners = lax.axis_size("tensor")
    replicas = lax.axis_size("dp")
    per = local_width // block
    own = nonzero // replicas
    column_hot = (
        column_of_slot[:, None] == jnp.arange(column_count, dtype=jnp.int32)[None, :]
    ).astype(jnp.int32)
    rows_gate = jnp.sum(column_hot[:, :, None] * gate_rows[None, :, :], axis=1)
    rows_up = jnp.sum(column_hot[:, :, None] * up_rows[None, :, :], axis=1)
    in_use = (column_of_slot < column_count).astype(jnp.bfloat16)

    x_local = tokens_in.reshape(tokens, per, block).transpose(1, 0, 2)
    hid = (hidden_grad * in_use[None, :, None]).transpose(1, 0, 2)
    x_all, hid_all = gather_all(x_local, hid)

    index = lax.axis_index("dp")
    own_gate = lax.dynamic_slice_in_dim(rows_gate, index * own, own, axis=1)
    own_up = lax.dynamic_slice_in_dim(rows_up, index * own, own, axis=1)

    cots, total = slots_call(
        rows_gate, rows_up, index.reshape(1).astype(jnp.int32), x_all, hid_all, gate_blocks, up_blocks
    )
    arrived = lax.all_to_all(
        total.reshape(owners, per, tokens, block), "tensor", split_axis=0, concat_axis=0, tiled=True
    )
    tokens_grad = (
        jnp.sum(arrived.astype(jnp.float32), axis=0)
        .astype(jnp.bfloat16)
        .transpose(1, 0, 2)
        .reshape(tokens, local_width)
    )
    gate_grad, up_grad = grads_call(own_gate, own_up, x_all, cots)
    return (tokens_grad, gate_grad, up_grad)


def solution(mesh):
    placed = (
        P(("groups", "dp"), "tensor"),
        P(("groups", "dp"), "tensor", None),
        P("tensor", None, None, None),
        P("tensor", None, None, None),
        P(),
        P(),
        P("tensor"),
    )
    return jax.shard_map(
        body,
        mesh=mesh,
        in_specs=placed,
        out_specs=(
            P(("groups", "dp"), "tensor"),
            P("tensor", ("groups", "dp"), None, None),
            P("tensor", ("groups", "dp"), None, None),
        ),
        check_vma=False,
    )
```

```python
import functools

import jax
import jax.numpy as jnp
from jax import lax
from jax.experimental import pallas as pl
from jax.experimental.pallas import tpu as pltpu
from jax.sharding import PartitionSpec as P

VMEM_LIMIT = 48 * 1024 * 1024
MESH = pl.DeviceIdType.MESH


def gather_kernel(owners, x_ref, hid_ref, xall_ref, hall_ref, send_x, recv_x, send_h, recv_h,
                  send_z, recv_z, send_sx, recv_sx, send_sh, recv_sh, local_sem):
    me = lax.axis_index("tensor")
    rep = lax.axis_index("dp")
    sib = rep + 1 - 2 * lax.rem(rep, 2)
    far = lax.rem(rep + 2, 4)
    slots = hid_ref.shape[0]
    half = slots // 2
    mine = lax.rem(rep, 2)
    theirs = 1 - mine
    has_left, has_right = me > 0, me < owners - 1

    barrier = pltpu.get_barrier_semaphore()
    pl.semaphore_signal(barrier, inc=1, device_id={"dp": sib}, device_id_type=MESH)
    pl.semaphore_signal(barrier, inc=1, device_id={"dp": far}, device_id_type=MESH)

    @pl.when(has_left)
    def _():
        pl.semaphore_signal(barrier, inc=1, device_id={"tensor": me - 1}, device_id_type=MESH)

    @pl.when(has_right)
    def _():
        pl.semaphore_signal(barrier, inc=1, device_id={"tensor": me + 1}, device_id_type=MESH)

    inner = jnp.where(has_left, 1, 0) + jnp.where(has_right, 1, 0)
    pl.semaphore_wait(barrier, 2 + inner)

    def remote(src, dst, send, recv, where):
        return pltpu.make_async_remote_copy(
            src_ref=src, dst_ref=dst, send_sem=send, recv_sem=recv,
            device_id=where, device_id_type=MESH,
        )

    home = (rep, far)
    from_sib = (sib, lax.rem(sib + 2, 4))

    def far_x(d):
        return remote(x_ref, xall_ref.at[me, d], send_x, recv_x, {"dp": far})

    def far_h(d, piece):
        span = pl.ds(piece * half, half)
        return remote(hid_ref.at[span], hall_ref.at[d, span], send_h.at[piece], recv_h.at[piece], {"dp": far})

    def sib_x(cls, z, owner):
        src = x_ref if (cls == 0 and z is me) else xall_ref.at[z, owner[cls]]
        return remote(src, xall_ref.at[z, owner[cls]], send_sx.at[cls, z], recv_sx.at[cls, z], {"dp": sib})

    def sib_h(cls, piece, owner):
        span = pl.ds(piece * half, half)
        src = hid_ref.at[span] if cls == 0 else hall_ref.at[owner[cls], span]
        return remote(src, hall_ref.at[owner[cls], span], send_sh.at[cls], recv_sh.at[cls], {"dp": sib})

    def along(way, cls, hop, z, to):
        src = x_ref if (cls == 0 and hop == 1) else xall_ref.at[z, home[cls]]
        return remote(src, xall_ref.at[z, home[cls]], send_z.at[way, cls, hop - 1], recv_z.at[way, cls, hop - 1], {"tensor": to})

    def out(way, cls, hop, act):
        step = 1 - 2 * way
        z = me - step * (hop - 1)
        to = me + step
        ok = jnp.logical_and(jnp.logical_and(to >= 0, to < owners), jnp.logical_and(z >= 0, z < owners))

        @pl.when(ok)
        def _():
            act(along(way, cls, hop, jnp.clip(z, 0, owners - 1), jnp.clip(to, 0, owners - 1)))

    def arrive(way, cls, hop):
        step = 1 - 2 * way
        z = me - step * hop

        @pl.when(jnp.logical_and(z >= 0, z < owners))
        def _():
            zc = jnp.clip(z, 0, owners - 1)
            frm = jnp.clip(me - step, 0, owners - 1)
            along(way, cls, hop, zc, frm).wait_recv()
            sib_x(cls, zc, home).start()

    own_x = pltpu.make_async_copy(x_ref, xall_ref.at[me, rep], local_sem.at[0])
    own_h = pltpu.make_async_copy(hid_ref, hall_ref.at[rep], local_sem.at[1])

    far_x(rep).start()
    for way in range(2):
        out(way, 0, 1, lambda c: c.start())
    sib_x(0, me, home).start()
    far_h(rep, theirs).start()
    far_h(rep, mine).start()
    sib_h(0, theirs, home).start()
    own_x.start()
    own_h.start()
    far_x(far).wait_recv()
    for way in range(2):
        out(way, 1, 1, lambda c: c.start())
    sib_x(1, me, home).start()
    for hop in range(1, owners):
        for cls in range(2):
            for way in range(2):
                arrive(way, cls, hop)
                if hop + 1 < owners:
                    out(way, cls, hop + 1, lambda c: c.start())
        if hop == 2 or owners == 2:
            far_h(far, theirs).wait_recv()
            sib_h(1, theirs, home).start()

    own_x.wait()
    own_h.wait()
    far_x(rep).wait_send()
    far_h(far, mine).wait_recv()
    for piece in range(2):
        far_h(rep, piece).wait_send()
    for hop in range(1, owners):
        for cls in range(2):
            for way in range(2):
                out(way, cls, hop, lambda c: c.wait_send())
    for cls in range(2):
        sib_h(cls, theirs, home).wait_send()
        sib_h(cls, mine, from_sib).wait_recv()
        for z in range(owners):
            sib_x(cls, z, home).wait_send()
            sib_x(cls, z, from_sib).wait_recv()


def gather_all(x_local, hid):
    owners = lax.axis_size("tensor")
    replicas = lax.axis_size("dp")
    if replicas != 4 or owners < 2 or owners > 8 or hid.shape[0] % 2:
        x_all = lax.all_gather(lax.all_gather(x_local, "dp", axis=0), "tensor", axis=0)
        return x_all, lax.all_gather(hid, "dp", axis=0)
    dma = pltpu.SemaphoreType.DMA
    hops = owners - 1
    return pl.pallas_call(
        functools.partial(gather_kernel, owners),
        in_specs=[pl.BlockSpec(memory_space=pl.ANY)] * 2,
        out_specs=[pl.BlockSpec(memory_space=pl.ANY)] * 2,
        out_shape=[
            jax.ShapeDtypeStruct((owners, replicas) + x_local.shape, x_local.dtype),
            jax.ShapeDtypeStruct((replicas,) + hid.shape, hid.dtype),
        ],
        scratch_shapes=[
            dma, dma, dma((2,)), dma((2,)),
            dma((2, 2, hops)), dma((2, 2, hops)),
            dma((2, owners)), dma((2, owners)),
            dma((2,)), dma((2,)), dma((2,)),
        ],
        compiler_params=pltpu.CompilerParams(collective_id=0, has_side_effects=True),
    )(x_local, hid)


def slot_kernel(nonzero, rows_gate, rows_up, where, x_ref, hid_ref, wg_ref, wu_ref, cot_ref, keep_ref, give_ref, acc_ref):
    step = pl.program_id(0)
    slot = where[1] + step

    @pl.when(step == 0)
    def _():
        acc_ref[...] = jnp.zeros_like(acc_ref)

    per = x_ref.shape[2]
    tokens = x_ref.shape[3]
    block = wg_ref.shape[-1]
    depth = nonzero * block
    rep = where[0]

    def product(rows, w_ref):
        parts = []
        for k in range(nonzero):
            row = rows[slot, k]
            owner = lax.div(row, per)
            parts.append(x_ref[owner, :, row - owner * per].reshape(-1, block))
        return jnp.dot(
            jnp.concatenate(parts, axis=1), w_ref[0].reshape(depth, block),
            preferred_element_type=jnp.float32,
        )

    gate = product(rows_gate, wg_ref)
    up = product(rows_up, wu_ref)
    hid = hid_ref[:, 0].reshape(-1, block).astype(jnp.float32)
    p = jax.nn.sigmoid(gate)
    gate_cot = (hid * up * p * (1.0 + gate * (1.0 - p))).astype(jnp.bfloat16)
    up_cot = (hid * gate * p).astype(jnp.bfloat16)
    cot_ref[0, 0] = gate_cot
    cot_ref[0, 1] = up_cot
    core = lax.rem(rep, 2)
    pair = pl.ds(pl.multiple_of((rep - core) * tokens, 2 * tokens), 2 * tokens)
    for which, (rows, w_ref) in enumerate(((rows_gate, wg_ref), (rows_up, wu_ref))):
        cot = cot_ref[0, which, pair, :].T
        back = jnp.dot(w_ref[0].reshape(depth, block), cot, preferred_element_type=jnp.float32)
        for k in range(nonzero):
            acc_ref[rows[slot, k]] += back[k * block : (k + 1) * block]

    @pl.when(step == pl.num_programs(0) - 1)
    def _():
        own = pl.ds(pl.multiple_of(core * tokens, tokens), tokens)
        other = pl.ds(pl.multiple_of((1 - core) * tokens, tokens), tokens)
        for r in range(acc_ref.shape[0]):
            keep_ref[r] = acc_ref[r, :, own].T
            give_ref[r] = acc_ref[r, :, other].T.astype(jnp.bfloat16)


def slots_call(rows_gate, rows_up, where, x_all, hid_all, wg, wu):
    owners, replicas, per, tokens, block = x_all.shape
    slot_count, nonzero = wg.shape[0] // 2, wg.shape[1]
    row_blocks = owners * per
    weight = pl.BlockSpec((1, nonzero, block, block), lambda i, a, b, c: (c[1] + i, 0, 0, 0))
    grad_spec = pl.BlockSpec((row_blocks, tokens, block), lambda i, a, b, c: (0, 0, 0))
    return pl.pallas_call(
        functools.partial(slot_kernel, nonzero),
        grid_spec=pltpu.PrefetchScalarGridSpec(
            num_scalar_prefetch=3,
            grid=(slot_count,),
            in_specs=[
                pl.BlockSpec(x_all.shape, lambda i, a, b, c: (0, 0, 0, 0, 0)),
                pl.BlockSpec((replicas, 1, tokens, block), lambda i, a, b, c: (0, c[1] + i, 0, 0)),
                weight,
                weight,
            ],
            out_specs=[
                pl.BlockSpec((1, 2, replicas * tokens, block), lambda i, a, b, c: (i, 0, 0, 0)),
                grad_spec,
                grad_spec,
            ],
            scratch_shapes=[pltpu.VMEM((row_blocks, block, 2 * tokens), jnp.float32)],
        ),
        out_shape=[
            jax.ShapeDtypeStruct((slot_count, 2, replicas * tokens, block), jnp.bfloat16),
            jax.ShapeDtypeStruct((row_blocks, tokens, block), jnp.float32),
            jax.ShapeDtypeStruct((row_blocks, tokens, block), jnp.bfloat16),
        ],
        compiler_params=pltpu.CompilerParams(
            dimension_semantics=("arbitrary",), vmem_limit_bytes=VMEM_LIMIT
        ),
        cost_estimate=pl.CostEstimate(
            flops=slot_count * nonzero * 2 * 6 * 2 * tokens * block * block,
            bytes_accessed=slot_count * nonzero * 4 * block * block,
            transcendentals=0,
        ),
    )(rows_gate, rows_up, where, x_all, hid_all, wg, wu)


def grad_kernel(rows_gate, rows_up, where, x_ref, cot_ref, *rest):
    gg_ref, gu_ref, xt_ref = rest[-3:]
    step = pl.program_id(0)
    slot = where[0] + step
    owners, _, per, _, block = x_ref.shape
    own = gg_ref.shape[1]

    @pl.when(step == 0)
    def _():
        for t in range(owners):
            for i in range(per):
                xt_ref[t * per + i] = x_ref[t, :, i].reshape(-1, block).T

    for which, (rows, out_ref) in enumerate(((rows_gate, gg_ref), (rows_up, gu_ref))):
        lhs = jnp.concatenate([xt_ref[rows[slot, k]] for k in range(own)], axis=0)
        both = jnp.dot(lhs, cot_ref[0, which], preferred_element_type=jnp.float32)
        out_ref[0] = both.reshape(own, block, block).astype(jnp.bfloat16)


def grads_call(rows_gate, rows_up, where, x_all, cots, before):
    slot_count, own = rows_gate.shape
    owners, replicas, per, tokens, block = x_all.shape
    count = cots.shape[0]
    out = jax.ShapeDtypeStruct((slot_count, own, block, block), jnp.bfloat16)
    out_spec = pl.BlockSpec((1, own, block, block), lambda i, a, b, c: (c[0] + i, 0, 0, 0))
    return pl.pallas_call(
        grad_kernel,
        grid_spec=pltpu.PrefetchScalarGridSpec(
            num_scalar_prefetch=3,
            grid=(count,),
            in_specs=[
                pl.BlockSpec(x_all.shape, lambda i, a, b, c: (0, 0, 0, 0, 0)),
                pl.BlockSpec((1, 2, replicas * tokens, block), lambda i, a, b, c: (i, 0, 0, 0)),
            ]
            + [pl.BlockSpec(memory_space=pl.ANY)] * len(before),
            out_specs=[out_spec, out_spec],
            scratch_shapes=[pltpu.VMEM((owners * per, block, replicas * tokens), jnp.bfloat16)],
        ),
        out_shape=[out, out],
        input_output_aliases={5: 0, 6: 1} if before else {},
        compiler_params=pltpu.CompilerParams(
            dimension_semantics=("arbitrary",), vmem_limit_bytes=VMEM_LIMIT
        ),
        cost_estimate=pl.CostEstimate(
            flops=count * own * 2 * 2 * replicas * tokens * block * block,
            bytes_accessed=count * own * 4 * block * block,
            transcendentals=0,
        ),
    )(rows_gate, rows_up, where, x_all, cots, *before)


def body(tokens_in, hidden_grad, gate_blocks, up_blocks, gate_rows, up_rows, column_of_slot):
    tokens, local_width = tokens_in.shape
    slot_count, nonzero, block = gate_blocks.shape[:3]
    column_count = gate_rows.shape[0]
    owners = lax.axis_size("tensor")
    replicas = lax.axis_size("dp")
    per = local_width // block
    own = nonzero // replicas
    column_hot = (
        column_of_slot[:, None] == jnp.arange(column_count, dtype=jnp.int32)[None, :]
    ).astype(jnp.int32)
    rows_gate = jnp.sum(column_hot[:, :, None] * gate_rows[None, :, :], axis=1)
    rows_up = jnp.sum(column_hot[:, :, None] * up_rows[None, :, :], axis=1)
    in_use = (column_of_slot < column_count).astype(jnp.bfloat16)

    x_local = tokens_in.reshape(tokens, per, block).transpose(1, 0, 2)
    hid = (hidden_grad * in_use[None, :, None]).transpose(1, 0, 2)
    x_all, hid_all = gather_all(x_local, hid)

    index = lax.axis_index("dp")
    own_gate = lax.dynamic_slice_in_dim(rows_gate, index * own, own, axis=1)
    own_up = lax.dynamic_slice_in_dim(rows_up, index * own, own, axis=1)

    half = slot_count // 2
    core = lax.rem(index, 2)
    first = (core * half).reshape(1).astype(jnp.int32)
    second = half - first
    where = jnp.stack([index.astype(jnp.int32), first[0]])
    swap = [(i, i + 1 - 2 * (i % 2)) for i in range(replicas)]
    cots, keep, give = slots_call(
        rows_gate, rows_up, where, x_all, hid_all, gate_blocks, up_blocks
    )
    got = lax.ppermute(give, "dp", swap)
    total = (keep + got.astype(jnp.float32)).astype(jnp.bfloat16)
    total, cots = lax.optimization_barrier((total, cots))
    sib_cots = lax.ppermute(cots, "dp", swap)
    arrived = lax.all_to_all(
        total.reshape(owners, per, tokens, block), "tensor", split_axis=0, concat_axis=0, tiled=True
    )
    tokens_grad = (
        jnp.sum(arrived.astype(jnp.float32), axis=0)
        .astype(jnp.bfloat16)
        .transpose(1, 0, 2)
        .reshape(tokens, local_width)
    )
    grads = grads_call(own_gate, own_up, first, x_all, cots, ())
    gate_grad, up_grad = grads_call(own_gate, own_up, second, x_all, sib_cots, grads)
    return (tokens_grad, gate_grad, up_grad)


def solution(mesh):
    placed = (
        P(("groups", "dp"), "tensor"),
        P(("groups", "dp"), "tensor", None),
        P("tensor", None, None, None),
        P("tensor", None, None, None),
        P(),
        P(),
        P("tensor"),
    )
    return jax.shard_map(
        body,
        mesh=mesh,
        in_specs=placed,
        out_specs=(
            P(("groups", "dp"), "tensor"),
            P("tensor", ("groups", "dp"), None, None),
            P("tensor", ("groups", "dp"), None, None),
        ),
        check_vma=False,
    )
```

```python
import functools

import jax
import jax.numpy as jnp
from jax import lax
from jax.experimental import pallas as pl
from jax.experimental.pallas import tpu as pltpu
from jax.sharding import PartitionSpec as P

VMEM_LIMIT = 48 * 1024 * 1024
MESH = pl.DeviceIdType.MESH


def gather_kernel(owners, x_ref, hid_ref, xall_ref, hall_ref, send_x, recv_x, send_h, recv_h,
                  send_z, recv_z, send_sx, recv_sx, send_sh, recv_sh, local_sem):
    me = lax.axis_index("tensor")
    rep = lax.axis_index("dp")
    sib = rep + 1 - 2 * lax.rem(rep, 2)
    far = lax.rem(rep + 2, 4)
    slots = hid_ref.shape[0]
    half = slots // 2
    mine = lax.rem(rep, 2)
    theirs = 1 - mine
    has_left, has_right = me > 0, me < owners - 1

    barrier = pltpu.get_barrier_semaphore()
    pl.semaphore_signal(barrier, inc=1, device_id={"dp": sib}, device_id_type=MESH)
    pl.semaphore_signal(barrier, inc=1, device_id={"dp": far}, device_id_type=MESH)

    @pl.when(has_left)
    def _():
        pl.semaphore_signal(barrier, inc=1, device_id={"tensor": me - 1}, device_id_type=MESH)

    @pl.when(has_right)
    def _():
        pl.semaphore_signal(barrier, inc=1, device_id={"tensor": me + 1}, device_id_type=MESH)

    inner = jnp.where(has_left, 1, 0) + jnp.where(has_right, 1, 0)
    pl.semaphore_wait(barrier, 2 + inner)

    def remote(src, dst, send, recv, where):
        return pltpu.make_async_remote_copy(
            src_ref=src, dst_ref=dst, send_sem=send, recv_sem=recv,
            device_id=where, device_id_type=MESH,
        )

    home = (rep, far)
    from_sib = (sib, lax.rem(sib + 2, 4))

    def far_x(d):
        return remote(x_ref, xall_ref.at[me, d], send_x, recv_x, {"dp": far})

    def far_h(d, piece):
        span = pl.ds(piece * half, half)
        return remote(hid_ref.at[span], hall_ref.at[d, span], send_h.at[piece], recv_h.at[piece], {"dp": far})

    def sib_x(cls, z, owner):
        src = x_ref if (cls == 0 and z is me) else xall_ref.at[z, owner[cls]]
        return remote(src, xall_ref.at[z, owner[cls]], send_sx.at[cls, z], recv_sx.at[cls, z], {"dp": sib})

    def sib_h(cls, piece, owner):
        span = pl.ds(piece * half, half)
        src = hid_ref.at[span] if cls == 0 else hall_ref.at[owner[cls], span]
        return remote(src, hall_ref.at[owner[cls], span], send_sh.at[cls], recv_sh.at[cls], {"dp": sib})

    def along(way, cls, hop, z, to):
        src = x_ref if (cls == 0 and hop == 1) else xall_ref.at[z, home[cls]]
        return remote(src, xall_ref.at[z, home[cls]], send_z.at[way, cls, hop - 1], recv_z.at[way, cls, hop - 1], {"tensor": to})

    def out(way, cls, hop, act):
        step = 1 - 2 * way
        z = me - step * (hop - 1)
        to = me + step
        ok = jnp.logical_and(jnp.logical_and(to >= 0, to < owners), jnp.logical_and(z >= 0, z < owners))

        @pl.when(ok)
        def _():
            act(along(way, cls, hop, jnp.clip(z, 0, owners - 1), jnp.clip(to, 0, owners - 1)))

    def arrive(way, cls, hop):
        step = 1 - 2 * way
        z = me - step * hop

        @pl.when(jnp.logical_and(z >= 0, z < owners))
        def _():
            zc = jnp.clip(z, 0, owners - 1)
            frm = jnp.clip(me - step, 0, owners - 1)
            along(way, cls, hop, zc, frm).wait_recv()
            sib_x(cls, zc, home).start()

    own_x = pltpu.make_async_copy(x_ref, xall_ref.at[me, rep], local_sem.at[0])
    own_h = pltpu.make_async_copy(hid_ref, hall_ref.at[rep], local_sem.at[1])

    far_x(rep).start()
    for way in range(2):
        out(way, 0, 1, lambda c: c.start())
    sib_x(0, me, home).start()
    sib_h(0, theirs, home).start()
    own_x.start()
    own_h.start()
    far_x(far).wait_recv()
    for way in range(2):
        out(way, 1, 1, lambda c: c.start())
    sib_x(1, me, home).start()
    far_h(rep, theirs).start()
    far_h(rep, mine).start()
    for hop in range(1, owners):
        for cls in range(2):
            for way in range(2):
                arrive(way, cls, hop)
                if hop + 1 < owners:
                    out(way, cls, hop + 1, lambda c: c.start())
        if hop == 2 or owners == 2:
            far_h(far, theirs).wait_recv()
            sib_h(1, theirs, home).start()

    own_x.wait()
    own_h.wait()
    far_x(rep).wait_send()
    far_h(far, mine).wait_recv()
    for piece in range(2):
        far_h(rep, piece).wait_send()
    for hop in range(1, owners):
        for cls in range(2):
            for way in range(2):
                out(way, cls, hop, lambda c: c.wait_send())
    for cls in range(2):
        sib_h(cls, theirs, home).wait_send()
        sib_h(cls, mine, from_sib).wait_recv()
        for z in range(owners):
            sib_x(cls, z, home).wait_send()
            sib_x(cls, z, from_sib).wait_recv()


def gather_all(x_local, hid):
    owners = lax.axis_size("tensor")
    replicas = lax.axis_size("dp")
    if replicas != 4 or owners < 2 or owners > 8 or hid.shape[0] % 2:
        x_all = lax.all_gather(lax.all_gather(x_local, "dp", axis=0), "tensor", axis=0)
        return x_all, lax.all_gather(hid, "dp", axis=0)
    dma = pltpu.SemaphoreType.DMA
    hops = owners - 1
    return pl.pallas_call(
        functools.partial(gather_kernel, owners),
        in_specs=[pl.BlockSpec(memory_space=pl.ANY)] * 2,
        out_specs=[pl.BlockSpec(memory_space=pl.ANY)] * 2,
        out_shape=[
            jax.ShapeDtypeStruct((owners, replicas) + x_local.shape, x_local.dtype),
            jax.ShapeDtypeStruct((replicas,) + hid.shape, hid.dtype),
        ],
        scratch_shapes=[
            dma, dma, dma((2,)), dma((2,)),
            dma((2, 2, hops)), dma((2, 2, hops)),
            dma((2, owners)), dma((2, owners)),
            dma((2,)), dma((2,)), dma((2,)),
        ],
        compiler_params=pltpu.CompilerParams(collective_id=0, has_side_effects=True),
    )(x_local, hid)


def slot_kernel(nonzero, rows_gate, rows_up, where, x_ref, hid_ref, wg_ref, wu_ref, cot_ref, keep_ref, give_ref, acc_ref):
    step = pl.program_id(0)
    slot = where[1] + step

    @pl.when(step == 0)
    def _():
        acc_ref[...] = jnp.zeros_like(acc_ref)

    block = wg_ref.shape[-1]
    tokens = x_ref.shape[2]
    per = x_ref.shape[3] // block
    depth = nonzero * block
    rep = where[0]

    def product(rows, w_ref):
        parts = []
        for k in range(nonzero):
            row = rows[slot, k]
            owner = lax.div(row, per)
            lanes = pl.ds(pl.multiple_of((row - owner * per) * block, block), block)
            parts.append(x_ref[owner, :, :, lanes].reshape(-1, block))
        return jnp.dot(
            jnp.concatenate(parts, axis=1), w_ref[0].reshape(depth, block),
            preferred_element_type=jnp.float32,
        )

    gate = product(rows_gate, wg_ref)
    up = product(rows_up, wu_ref)
    hid = hid_ref[:, 0].reshape(-1, block).astype(jnp.float32)
    p = jax.nn.sigmoid(gate)
    gate_cot = (hid * up * p * (1.0 + gate * (1.0 - p))).astype(jnp.bfloat16)
    up_cot = (hid * gate * p).astype(jnp.bfloat16)
    cot_ref[0, 0] = gate_cot
    cot_ref[0, 1] = up_cot
    core = lax.rem(rep, 2)
    pair = pl.ds(pl.multiple_of((rep - core) * tokens, 2 * tokens), 2 * tokens)
    for which, (rows, w_ref) in enumerate(((rows_gate, wg_ref), (rows_up, wu_ref))):
        cot = cot_ref[0, which, pair, :].T
        back = jnp.dot(w_ref[0].reshape(depth, block), cot, preferred_element_type=jnp.float32)
        for k in range(nonzero):
            acc_ref[rows[slot, k]] += back[k * block : (k + 1) * block]

    @pl.when(step == pl.num_programs(0) - 1)
    def _():
        own = pl.ds(pl.multiple_of(core * tokens, tokens), tokens)
        other = pl.ds(pl.multiple_of((1 - core) * tokens, tokens), tokens)
        for r in range(acc_ref.shape[0]):
            lanes = pl.ds((r % per) * block, block)
            keep_ref[r // per, :, lanes] = acc_ref[r, :, own].T
            give_ref[r // per, :, lanes] = acc_ref[r, :, other].T.astype(jnp.bfloat16)


def slots_call(rows_gate, rows_up, where, x_all, hid_all, wg, wu):
    owners, replicas, tokens, width = x_all.shape
    block = wg.shape[-1]
    slot_count, nonzero = wg.shape[0] // 2, wg.shape[1]
    row_blocks = owners * width // block
    weight = pl.BlockSpec((1, nonzero, block, block), lambda i, a, b, c: (c[1] + i, 0, 0, 0))
    grad_spec = pl.BlockSpec((owners, tokens, width), lambda i, a, b, c: (0, 0, 0))
    return pl.pallas_call(
        functools.partial(slot_kernel, nonzero),
        grid_spec=pltpu.PrefetchScalarGridSpec(
            num_scalar_prefetch=3,
            grid=(slot_count,),
            in_specs=[
                pl.BlockSpec(x_all.shape, lambda i, a, b, c: (0, 0, 0, 0)),
                pl.BlockSpec((replicas, 1, tokens, block), lambda i, a, b, c: (0, c[1] + i, 0, 0)),
                weight,
                weight,
            ],
            out_specs=[
                pl.BlockSpec((1, 2, replicas * tokens, block), lambda i, a, b, c: (i, 0, 0, 0)),
                grad_spec,
                grad_spec,
            ],
            scratch_shapes=[pltpu.VMEM((row_blocks, block, 2 * tokens), jnp.float32)],
        ),
        out_shape=[
            jax.ShapeDtypeStruct((slot_count, 2, replicas * tokens, block), jnp.bfloat16),
            jax.ShapeDtypeStruct((owners, tokens, width), jnp.float32),
            jax.ShapeDtypeStruct((owners, tokens, width), jnp.bfloat16),
        ],
        compiler_params=pltpu.CompilerParams(
            dimension_semantics=("arbitrary",), vmem_limit_bytes=VMEM_LIMIT
        ),
        cost_estimate=pl.CostEstimate(
            flops=slot_count * nonzero * 2 * 6 * 2 * tokens * block * block,
            bytes_accessed=slot_count * nonzero * 4 * block * block,
            transcendentals=0,
        ),
    )(rows_gate, rows_up, where, x_all, hid_all, wg, wu)


def grad_kernel(rows_gate, rows_up, where, x_ref, cot_ref, *rest):
    later = len(rest) > 3
    gg_ref, gu_ref = rest[2:4] if later else rest[:2]
    xt_ref = x_ref if later else rest[2]
    step = pl.program_id(0)
    slot = where[0] + step
    own, block = gg_ref.shape[1], gg_ref.shape[-1]

    if not later:

        @pl.when(step == 0)
        def _():
            per = x_ref.shape[3] // block
            for r in range(xt_ref.shape[0]):
                lanes = pl.ds((r % per) * block, block)
                xt_ref[r] = x_ref[r // per, :, :, lanes].reshape(-1, block).T

    for which, (rows, out_ref) in enumerate(((rows_gate, gg_ref), (rows_up, gu_ref))):
        lhs = jnp.concatenate([xt_ref[rows[slot, k]] for k in range(own)], axis=0)
        both = jnp.dot(lhs, cot_ref[0, which], preferred_element_type=jnp.float32)
        out_ref[0] = both.reshape(own, block, block).astype(jnp.bfloat16)


def grads_call(rows_gate, rows_up, where, x, cots, before):
    slot_count, own = rows_gate.shape
    count, _, tokens, block = cots.shape
    out = jax.ShapeDtypeStruct((slot_count, own, block, block), jnp.bfloat16)
    out_spec = pl.BlockSpec((1, own, block, block), lambda i, a, b, c: (c[0] + i, 0, 0, 0))
    out_shape, out_specs = [out, out], [out_spec, out_spec]
    if not before:
        row_blocks = x.shape[0] * x.shape[3] // block
        out_shape.append(jax.ShapeDtypeStruct((row_blocks, block, tokens), jnp.bfloat16))
        out_specs.append(pl.BlockSpec((row_blocks, block, tokens), lambda i, a, b, c: (0, 0, 0)))
    return pl.pallas_call(
        grad_kernel,
        grid_spec=pltpu.PrefetchScalarGridSpec(
            num_scalar_prefetch=3,
            grid=(count,),
            in_specs=[
                pl.BlockSpec(x.shape, lambda i, a, b, c: (0,) * x.ndim),
                pl.BlockSpec((1, 2, tokens, block), lambda i, a, b, c: (i, 0, 0, 0)),
            ]
            + [pl.BlockSpec(memory_space=pl.ANY)] * len(before),
            out_specs=out_specs,
        ),
        out_shape=out_shape,
        input_output_aliases={5: 0, 6: 1} if before else {},
        compiler_params=pltpu.CompilerParams(
            dimension_semantics=("arbitrary",), vmem_limit_bytes=VMEM_LIMIT
        ),
        cost_estimate=pl.CostEstimate(
            flops=count * own * 2 * 2 * block * block,
            bytes_accessed=count * own * 4 * block,
            transcendentals=0,
        ),
    )(rows_gate, rows_up, where, x, cots, *before)


def body(tokens_in, hidden_grad, gate_blocks, up_blocks, gate_rows, up_rows, column_of_slot):
    slot_count, nonzero = gate_blocks.shape[:2]
    column_count = gate_rows.shape[0]
    replicas = lax.axis_size("dp")
    own = nonzero // replicas
    column_hot = (
        column_of_slot[:, None] == jnp.arange(column_count, dtype=jnp.int32)[None, :]
    ).astype(jnp.int32)
    rows_gate = jnp.sum(column_hot[:, :, None] * gate_rows[None, :, :], axis=1)
    rows_up = jnp.sum(column_hot[:, :, None] * up_rows[None, :, :], axis=1)
    in_use = (column_of_slot < column_count).astype(jnp.bfloat16)

    hid = (hidden_grad * in_use[None, :, None]).transpose(1, 0, 2)
    x_all, hid_all = gather_all(tokens_in, hid)

    index = lax.axis_index("dp")
    own_gate = lax.dynamic_slice_in_dim(rows_gate, index * own, own, axis=1)
    own_up = lax.dynamic_slice_in_dim(rows_up, index * own, own, axis=1)

    half = slot_count // 2
    core = lax.rem(index, 2)
    first = (core * half).reshape(1).astype(jnp.int32)
    second = half - first
    where = jnp.stack([index.astype(jnp.int32), first[0]])
    swap = [(i, i + 1 - 2 * (i % 2)) for i in range(replicas)]
    cots, keep, give = slots_call(
        rows_gate, rows_up, where, x_all, hid_all, gate_blocks, up_blocks
    )
    got = lax.ppermute(give, "dp", swap)
    total = (keep + got.astype(jnp.float32)).astype(jnp.bfloat16)
    total, cots = lax.optimization_barrier((total, cots))
    sib_cots = lax.ppermute(cots, "dp", swap)
    arrived = lax.all_to_all(
        total, "tensor", split_axis=0, concat_axis=0, tiled=True
    )
    tokens_grad = jnp.sum(arrived.astype(jnp.float32), axis=0).astype(jnp.bfloat16)
    gate_grad, up_grad, x_turned = grads_call(own_gate, own_up, first, x_all, cots, ())
    gate_grad, up_grad = grads_call(own_gate, own_up, second, x_turned, sib_cots, (gate_grad, up_grad))
    return (tokens_grad, gate_grad, up_grad)


def solution(mesh):
    placed = (
        P(("groups", "dp"), "tensor"),
        P(("groups", "dp"), "tensor", None),
        P("tensor", None, None, None),
        P("tensor", None, None, None),
        P(),
        P(),
        P("tensor"),
    )
    return jax.shard_map(
        body,
        mesh=mesh,
        in_specs=placed,
        out_specs=(
            P(("groups", "dp"), "tensor"),
            P("tensor", ("groups", "dp"), None, None),
            P("tensor", ("groups", "dp"), None, None),
        ),
        check_vma=False,
    )
```

```python
import functools

import jax
import jax.numpy as jnp
from jax import lax
from jax.experimental import pallas as pl
from jax.experimental.pallas import tpu as pltpu
from jax.sharding import PartitionSpec as P

VMEM_LIMIT = 48 * 1024 * 1024
MESH = pl.DeviceIdType.MESH


def gather_kernel(owners, x_ref, hid_ref, xall_ref, hall_ref, send_x, recv_x, send_h, recv_h,
                  send_z, recv_z, send_sx, recv_sx, send_sh, recv_sh, local_sem):
    me = lax.axis_index("tensor")
    rep = lax.axis_index("dp")
    sib = rep + 1 - 2 * lax.rem(rep, 2)
    far = lax.rem(rep + 2, 4)
    slots = hid_ref.shape[0]
    half = slots // 2
    mine = lax.rem(rep, 2)
    theirs = 1 - mine
    has_left, has_right = me > 0, me < owners - 1

    barrier = pltpu.get_barrier_semaphore()
    pl.semaphore_signal(barrier, inc=1, device_id={"dp": sib}, device_id_type=MESH)
    pl.semaphore_signal(barrier, inc=1, device_id={"dp": far}, device_id_type=MESH)

    @pl.when(has_left)
    def _():
        pl.semaphore_signal(barrier, inc=1, device_id={"tensor": me - 1}, device_id_type=MESH)

    @pl.when(has_right)
    def _():
        pl.semaphore_signal(barrier, inc=1, device_id={"tensor": me + 1}, device_id_type=MESH)

    inner = jnp.where(has_left, 1, 0) + jnp.where(has_right, 1, 0)
    pl.semaphore_wait(barrier, 2 + inner)

    def remote(src, dst, send, recv, where):
        return pltpu.make_async_remote_copy(
            src_ref=src, dst_ref=dst, send_sem=send, recv_sem=recv,
            device_id=where, device_id_type=MESH,
        )

    home = (rep, far)
    from_sib = (sib, lax.rem(sib + 2, 4))

    def far_x(d):
        return remote(x_ref, xall_ref.at[me, d], send_x, recv_x, {"dp": far})

    def far_h(d, piece):
        span = pl.ds(piece * half, half)
        return remote(hid_ref.at[span], hall_ref.at[d, span], send_h.at[piece], recv_h.at[piece], {"dp": far})

    def sib_x(cls, z, owner):
        src = x_ref if (cls == 0 and z is me) else xall_ref.at[z, owner[cls]]
        return remote(src, xall_ref.at[z, owner[cls]], send_sx.at[cls, z], recv_sx.at[cls, z], {"dp": sib})

    def sib_h(cls, piece, owner):
        span = pl.ds(piece * half, half)
        src = hid_ref.at[span] if cls == 0 else hall_ref.at[owner[cls], span]
        return remote(src, hall_ref.at[owner[cls], span], send_sh.at[cls], recv_sh.at[cls], {"dp": sib})

    def along(way, cls, hop, z, to):
        src = x_ref if (cls == 0 and hop == 1) else xall_ref.at[z, home[cls]]
        return remote(src, xall_ref.at[z, home[cls]], send_z.at[way, cls, hop - 1], recv_z.at[way, cls, hop - 1], {"tensor": to})

    def out(way, cls, hop, act):
        step = 1 - 2 * way
        z = me - step * (hop - 1)
        to = me + step
        ok = jnp.logical_and(jnp.logical_and(to >= 0, to < owners), jnp.logical_and(z >= 0, z < owners))

        @pl.when(ok)
        def _():
            act(along(way, cls, hop, jnp.clip(z, 0, owners - 1), jnp.clip(to, 0, owners - 1)))

    def arrive(way, cls, hop):
        step = 1 - 2 * way
        z = me - step * hop

        @pl.when(jnp.logical_and(z >= 0, z < owners))
        def _():
            zc = jnp.clip(z, 0, owners - 1)
            frm = jnp.clip(me - step, 0, owners - 1)
            along(way, cls, hop, zc, frm).wait_recv()
            sib_x(cls, zc, home).start()

    own_x = pltpu.make_async_copy(x_ref, xall_ref.at[me, rep], local_sem.at[0])
    own_h = pltpu.make_async_copy(hid_ref, hall_ref.at[rep], local_sem.at[1])

    far_x(rep).start()
    for way in range(2):
        out(way, 0, 1, lambda c: c.start())
    sib_x(0, me, home).start()
    sib_h(0, theirs, home).start()
    own_x.start()
    own_h.start()
    far_x(far).wait_recv()
    for way in range(2):
        out(way, 1, 1, lambda c: c.start())
    sib_x(1, me, home).start()
    far_h(rep, theirs).start()
    far_h(rep, mine).start()
    for hop in range(1, owners):
        for cls in range(2):
            for way in range(2):
                arrive(way, cls, hop)
                if hop + 1 < owners:
                    out(way, cls, hop + 1, lambda c: c.start())
        if hop == 2 or owners == 2:
            far_h(far, theirs).wait_recv()
            sib_h(1, theirs, home).start()

    own_x.wait()
    own_h.wait()
    far_x(rep).wait_send()
    far_h(far, mine).wait_recv()
    for piece in range(2):
        far_h(rep, piece).wait_send()
    for hop in range(1, owners):
        for cls in range(2):
            for way in range(2):
                out(way, cls, hop, lambda c: c.wait_send())
    for cls in range(2):
        sib_h(cls, theirs, home).wait_send()
        sib_h(cls, mine, from_sib).wait_recv()
        for z in range(owners):
            sib_x(cls, z, home).wait_send()
            sib_x(cls, z, from_sib).wait_recv()


def gather_all(x_local, hid):
    owners = lax.axis_size("tensor")
    replicas = lax.axis_size("dp")
    if replicas != 4 or owners < 2 or owners > 8 or hid.shape[0] % 2:
        x_all = lax.all_gather(lax.all_gather(x_local, "dp", axis=0), "tensor", axis=0)
        return x_all, lax.all_gather(hid, "dp", axis=0)
    dma = pltpu.SemaphoreType.DMA
    hops = owners - 1
    return pl.pallas_call(
        functools.partial(gather_kernel, owners),
        in_specs=[pl.BlockSpec(memory_space=pl.ANY)] * 2,
        out_specs=[pl.BlockSpec(memory_space=pl.ANY)] * 2,
        out_shape=[
            jax.ShapeDtypeStruct((owners, replicas) + x_local.shape, x_local.dtype),
            jax.ShapeDtypeStruct((replicas,) + hid.shape, hid.dtype),
        ],
        scratch_shapes=[
            dma, dma, dma((2,)), dma((2,)),
            dma((2, 2, hops)), dma((2, 2, hops)),
            dma((2, owners)), dma((2, owners)),
            dma((2,)), dma((2,)), dma((2,)),
        ],
        compiler_params=pltpu.CompilerParams(collective_id=0, has_side_effects=True),
    )(x_local, hid)


def slot_kernel(nonzero, rows_gate, rows_up, where, x_ref, hid_ref, wg_ref, wu_ref, cot_ref, keep_ref, give_ref, acc_ref):
    step = pl.program_id(0)
    slot = where[1] + step

    @pl.when(step == 0)
    def _():
        acc_ref[...] = jnp.zeros_like(acc_ref)

    block = wg_ref.shape[-1]
    tokens = x_ref.shape[2]
    per = x_ref.shape[3] // block
    depth = nonzero * block
    rep = where[0]

    def product(rows, w_ref):
        parts = []
        for k in range(nonzero):
            row = rows[slot, k]
            owner = lax.div(row, per)
            lanes = pl.ds(pl.multiple_of((row - owner * per) * block, block), block)
            parts.append(x_ref[owner, :, :, lanes].reshape(-1, block))
        return jnp.dot(
            jnp.concatenate(parts, axis=1), w_ref[0].reshape(depth, block),
            preferred_element_type=jnp.float32,
        )

    gate = product(rows_gate, wg_ref)
    up = product(rows_up, wu_ref)
    hid = hid_ref[:, 0].reshape(-1, block).astype(jnp.float32)
    p = jax.nn.sigmoid(gate)
    gate_cot = (hid * up * p * (1.0 + gate * (1.0 - p))).astype(jnp.bfloat16)
    up_cot = (hid * gate * p).astype(jnp.bfloat16)
    cot_ref[0, 0] = gate_cot
    cot_ref[0, 1] = up_cot
    core = lax.rem(rep, 2)
    pair = pl.ds(pl.multiple_of((rep - core) * tokens, 2 * tokens), 2 * tokens)
    for which, (rows, w_ref) in enumerate(((rows_gate, wg_ref), (rows_up, wu_ref))):
        cot = cot_ref[0, which, pair, :].T
        back = jnp.dot(w_ref[0].reshape(depth, block), cot, preferred_element_type=jnp.float32)
        for k in range(nonzero):
            acc_ref[rows[slot, k]] += back[k * block : (k + 1) * block]

    @pl.when(step == pl.num_programs(0) - 1)
    def _():
        own = pl.ds(pl.multiple_of(core * tokens, tokens), tokens)
        other = pl.ds(pl.multiple_of((1 - core) * tokens, tokens), tokens)
        for r in range(acc_ref.shape[0]):
            lanes = pl.ds((r % per) * block, block)
            keep_ref[r // per, :, lanes] = acc_ref[r, :, own].T
            give_ref[r // per, :, lanes] = acc_ref[r, :, other].T.astype(jnp.bfloat16)


def slots_call(rows_gate, rows_up, where, x_all, hid_all, wg, wu):
    owners, replicas, tokens, width = x_all.shape
    block = wg.shape[-1]
    slot_count, nonzero = wg.shape[0] // 2, wg.shape[1]
    row_blocks = owners * width // block
    weight = pl.BlockSpec((1, nonzero, block, block), lambda i, a, b, c: (c[1] + i, 0, 0, 0))
    grad_spec = pl.BlockSpec((owners, tokens, width), lambda i, a, b, c: (0, 0, 0))
    return pl.pallas_call(
        functools.partial(slot_kernel, nonzero),
        grid_spec=pltpu.PrefetchScalarGridSpec(
            num_scalar_prefetch=3,
            grid=(slot_count,),
            in_specs=[
                pl.BlockSpec(x_all.shape, lambda i, a, b, c: (0, 0, 0, 0)),
                pl.BlockSpec((replicas, 1, tokens, block), lambda i, a, b, c: (0, c[1] + i, 0, 0)),
                weight,
                weight,
            ],
            out_specs=[
                pl.BlockSpec((1, 2, replicas * tokens, block), lambda i, a, b, c: (i, 0, 0, 0)),
                grad_spec,
                grad_spec,
            ],
            scratch_shapes=[pltpu.VMEM((row_blocks, block, 2 * tokens), jnp.float32)],
        ),
        out_shape=[
            jax.ShapeDtypeStruct((slot_count, 2, replicas * tokens, block), jnp.bfloat16),
            jax.ShapeDtypeStruct((owners, tokens, width), jnp.float32),
            jax.ShapeDtypeStruct((owners, tokens, width), jnp.bfloat16),
        ],
        compiler_params=pltpu.CompilerParams(
            dimension_semantics=("arbitrary",), vmem_limit_bytes=VMEM_LIMIT
        ),
        cost_estimate=pl.CostEstimate(
            flops=slot_count * nonzero * 2 * 6 * 2 * tokens * block * block,
            bytes_accessed=slot_count * nonzero * 4 * block * block,
            transcendentals=0,
        ),
    )(rows_gate, rows_up, where, x_all, hid_all, wg, wu)


def grad_slot(step, where, half):
    late = step >= half
    return jnp.where(late, half - where[0] + step - half, where[0] + step)


def grad_kernel(half, rows_gate, rows_up, where, x_ref, cot_ref, sib_ref, gg_ref, gu_ref, xt_ref):
    step = pl.program_id(0)
    slot = grad_slot(step, where, half)
    own, block = gg_ref.shape[1], gg_ref.shape[-1]

    @pl.when(step == 0)
    def _():
        per = x_ref.shape[3] // block
        for r in range(xt_ref.shape[0]):
            lanes = pl.ds((r % per) * block, block)
            xt_ref[r] = x_ref[r // per, :, :, lanes].reshape(-1, block).T

    def work(source):
        for which, (rows, out_ref) in enumerate(((rows_gate, gg_ref), (rows_up, gu_ref))):
            lhs = jnp.concatenate([xt_ref[rows[slot, k]] for k in range(own)], axis=0)
            both = jnp.dot(lhs, source[0, which], preferred_element_type=jnp.float32)
            out_ref[0] = both.reshape(own, block, block).astype(jnp.bfloat16)

    @pl.when(step < half)
    def _():
        work(cot_ref)

    @pl.when(step >= half)
    def _():
        work(sib_ref)


def grads_call(rows_gate, rows_up, where, x_all, cots, sib_cots):
    slot_count, own = rows_gate.shape
    half, _, tokens, block = cots.shape
    row_blocks = x_all.shape[0] * x_all.shape[3] // block
    out = jax.ShapeDtypeStruct((slot_count, own, block, block), jnp.bfloat16)
    out_spec = pl.BlockSpec(
        (1, own, block, block), lambda i, a, b, c: (grad_slot(i, c, half), 0, 0, 0)
    )
    return pl.pallas_call(
        functools.partial(grad_kernel, half),
        grid_spec=pltpu.PrefetchScalarGridSpec(
            num_scalar_prefetch=3,
            grid=(slot_count,),
            in_specs=[
                pl.BlockSpec(x_all.shape, lambda i, a, b, c: (0, 0, 0, 0)),
                pl.BlockSpec(
                    (1, 2, tokens, block), lambda i, a, b, c: (jnp.minimum(i, half - 1), 0, 0, 0)
                ),
                pl.BlockSpec(
                    (1, 2, tokens, block), lambda i, a, b, c: (jnp.maximum(i - half, 0), 0, 0, 0)
                ),
            ],
            out_specs=[out_spec, out_spec],
            scratch_shapes=[pltpu.VMEM((row_blocks, block, tokens), jnp.bfloat16)],
        ),
        out_shape=[out, out],
        compiler_params=pltpu.CompilerParams(
            dimension_semantics=("arbitrary",), vmem_limit_bytes=VMEM_LIMIT
        ),
        cost_estimate=pl.CostEstimate(
            flops=slot_count * own * 2 * 2 * tokens * block * block,
            bytes_accessed=slot_count * own * 4 * block * block,
            transcendentals=0,
        ),
    )(rows_gate, rows_up, where, x_all, cots, sib_cots)


def body(tokens_in, hidden_grad, gate_blocks, up_blocks, gate_rows, up_rows, column_of_slot):
    slot_count, nonzero = gate_blocks.shape[:2]
    column_count = gate_rows.shape[0]
    replicas = lax.axis_size("dp")
    own = nonzero // replicas
    column_hot = (
        column_of_slot[:, None] == jnp.arange(column_count, dtype=jnp.int32)[None, :]
    ).astype(jnp.int32)
    rows_gate = jnp.sum(column_hot[:, :, None] * gate_rows[None, :, :], axis=1)
    rows_up = jnp.sum(column_hot[:, :, None] * up_rows[None, :, :], axis=1)
    in_use = (column_of_slot < column_count).astype(jnp.bfloat16)

    hid = (hidden_grad * in_use[None, :, None]).transpose(1, 0, 2)
    x_all, hid_all = gather_all(tokens_in, hid)

    index = lax.axis_index("dp")
    own_gate = lax.dynamic_slice_in_dim(rows_gate, index * own, own, axis=1)
    own_up = lax.dynamic_slice_in_dim(rows_up, index * own, own, axis=1)

    half = slot_count // 2
    core = lax.rem(index, 2)
    first = (core * half).reshape(1).astype(jnp.int32)
    where = jnp.stack([index.astype(jnp.int32), first[0]])
    swap = [(i, i + 1 - 2 * (i % 2)) for i in range(replicas)]
    cots, keep, give = slots_call(
        rows_gate, rows_up, where, x_all, hid_all, gate_blocks, up_blocks
    )
    got = lax.ppermute(give, "dp", swap)
    total = (keep + got.astype(jnp.float32)).astype(jnp.bfloat16)
    sib_cots = lax.ppermute(cots, "dp", swap)
    arrived = lax.all_to_all(
        total, "tensor", split_axis=0, concat_axis=0, tiled=True
    )
    tokens_grad = jnp.sum(arrived.astype(jnp.float32), axis=0).astype(jnp.bfloat16)
    gate_grad, up_grad = grads_call(own_gate, own_up, first, x_all, cots, sib_cots)
    return (tokens_grad, gate_grad, up_grad)


def solution(mesh):
    placed = (
        P(("groups", "dp"), "tensor"),
        P(("groups", "dp"), "tensor", None),
        P("tensor", None, None, None),
        P("tensor", None, None, None),
        P(),
        P(),
        P("tensor"),
    )
    return jax.shard_map(
        body,
        mesh=mesh,
        in_specs=placed,
        out_specs=(
            P(("groups", "dp"), "tensor"),
            P("tensor", ("groups", "dp"), None, None),
            P("tensor", ("groups", "dp"), None, None),
        ),
        check_vma=False,
    )
```

```python
import functools

import jax
import jax.numpy as jnp
from jax import lax
from jax.experimental import pallas as pl
from jax.experimental.pallas import tpu as pltpu
from jax.sharding import PartitionSpec as P

VMEM_LIMIT = 48 * 1024 * 1024
MESH = pl.DeviceIdType.MESH


def gather_kernel(owners, x_ref, hid_ref, xall_ref, hall_ref, send_x, recv_x, send_h, recv_h,
                  send_z, recv_z, send_sx, recv_sx, send_sh, recv_sh, local_sem):
    me = lax.axis_index("tensor")
    rep = lax.axis_index("dp")
    sib = rep + 1 - 2 * lax.rem(rep, 2)
    far = lax.rem(rep + 2, 4)
    slots = hid_ref.shape[0]
    half = slots // 2
    mine = lax.rem(rep, 2)
    theirs = 1 - mine
    has_left, has_right = me > 0, me < owners - 1

    barrier = pltpu.get_barrier_semaphore()
    pl.semaphore_signal(barrier, inc=1, device_id={"dp": sib}, device_id_type=MESH)
    pl.semaphore_signal(barrier, inc=1, device_id={"dp": far}, device_id_type=MESH)

    @pl.when(has_left)
    def _():
        pl.semaphore_signal(barrier, inc=1, device_id={"tensor": me - 1}, device_id_type=MESH)

    @pl.when(has_right)
    def _():
        pl.semaphore_signal(barrier, inc=1, device_id={"tensor": me + 1}, device_id_type=MESH)

    inner = jnp.where(has_left, 1, 0) + jnp.where(has_right, 1, 0)
    pl.semaphore_wait(barrier, 2 + inner)

    def remote(src, dst, send, recv, where):
        return pltpu.make_async_remote_copy(
            src_ref=src, dst_ref=dst, send_sem=send, recv_sem=recv,
            device_id=where, device_id_type=MESH,
        )

    home = (rep, far)
    from_sib = (sib, lax.rem(sib + 2, 4))

    def far_x(d):
        return remote(x_ref, xall_ref.at[me, d], send_x, recv_x, {"dp": far})

    def far_h(d, piece):
        span = pl.ds(piece * half, half)
        return remote(hid_ref.at[span], hall_ref.at[d, span], send_h.at[piece], recv_h.at[piece], {"dp": far})

    def sib_x(cls, z, owner):
        src = x_ref if (cls == 0 and z is me) else xall_ref.at[z, owner[cls]]
        return remote(src, xall_ref.at[z, owner[cls]], send_sx.at[cls, z], recv_sx.at[cls, z], {"dp": sib})

    def sib_h(cls, piece, owner):
        span = pl.ds(piece * half, half)
        src = hid_ref.at[span] if cls == 0 else hall_ref.at[owner[cls], span]
        return remote(src, hall_ref.at[owner[cls], span], send_sh.at[cls], recv_sh.at[cls], {"dp": sib})

    def along(way, cls, hop, z, to):
        src = x_ref if (cls == 0 and hop == 1) else xall_ref.at[z, home[cls]]
        return remote(src, xall_ref.at[z, home[cls]], send_z.at[way, cls, hop - 1], recv_z.at[way, cls, hop - 1], {"tensor": to})

    def out(way, cls, hop, act):
        step = 1 - 2 * way
        z = me - step * (hop - 1)
        to = me + step
        ok = jnp.logical_and(jnp.logical_and(to >= 0, to < owners), jnp.logical_and(z >= 0, z < owners))

        @pl.when(ok)
        def _():
            act(along(way, cls, hop, jnp.clip(z, 0, owners - 1), jnp.clip(to, 0, owners - 1)))

    def arrive(way, cls, hop):
        step = 1 - 2 * way
        z = me - step * hop

        @pl.when(jnp.logical_and(z >= 0, z < owners))
        def _():
            zc = jnp.clip(z, 0, owners - 1)
            frm = jnp.clip(me - step, 0, owners - 1)
            along(way, cls, hop, zc, frm).wait_recv()
            sib_x(cls, zc, home).start()

    own_x = pltpu.make_async_copy(x_ref, xall_ref.at[me, rep], local_sem.at[0])
    own_h = pltpu.make_async_copy(hid_ref, hall_ref.at[rep], local_sem.at[1])

    far_x(rep).start()
    for way in range(2):
        out(way, 0, 1, lambda c: c.start())
    sib_x(0, me, home).start()
    sib_h(0, theirs, home).start()
    own_x.start()
    own_h.start()
    far_x(far).wait_recv()
    for way in range(2):
        out(way, 1, 1, lambda c: c.start())
    sib_x(1, me, home).start()
    far_h(rep, theirs).start()
    far_h(rep, mine).start()
    for hop in range(1, owners):
        for cls in range(2):
            for way in range(2):
                arrive(way, cls, hop)
                if hop + 1 < owners:
                    out(way, cls, hop + 1, lambda c: c.start())
        if hop == 2 or owners == 2:
            far_h(far, theirs).wait_recv()
            sib_h(1, theirs, home).start()

    own_x.wait()
    own_h.wait()
    far_x(rep).wait_send()
    far_h(far, mine).wait_recv()
    for piece in range(2):
        far_h(rep, piece).wait_send()
    for hop in range(1, owners):
        for cls in range(2):
            for way in range(2):
                out(way, cls, hop, lambda c: c.wait_send())
    for cls in range(2):
        sib_h(cls, theirs, home).wait_send()
        sib_h(cls, mine, from_sib).wait_recv()
        for z in range(owners):
            sib_x(cls, z, home).wait_send()
            sib_x(cls, z, from_sib).wait_recv()


def gather_all(x_local, hid):
    owners = lax.axis_size("tensor")
    replicas = lax.axis_size("dp")
    if replicas != 4 or owners < 2 or owners > 8 or hid.shape[0] % 2:
        x_all = lax.all_gather(lax.all_gather(x_local, "dp", axis=0), "tensor", axis=0)
        return x_all, lax.all_gather(hid, "dp", axis=0)
    dma = pltpu.SemaphoreType.DMA
    hops = owners - 1
    return pl.pallas_call(
        functools.partial(gather_kernel, owners),
        in_specs=[pl.BlockSpec(memory_space=pl.ANY)] * 2,
        out_specs=[pl.BlockSpec(memory_space=pl.ANY)] * 2,
        out_shape=[
            jax.ShapeDtypeStruct((owners, replicas) + x_local.shape, x_local.dtype),
            jax.ShapeDtypeStruct((replicas,) + hid.shape, hid.dtype),
        ],
        scratch_shapes=[
            dma, dma, dma((2,)), dma((2,)),
            dma((2, 2, hops)), dma((2, 2, hops)),
            dma((2, owners)), dma((2, owners)),
            dma((2,)), dma((2,)), dma((2,)),
        ],
        compiler_params=pltpu.CompilerParams(collective_id=0, has_side_effects=True),
    )(x_local, hid)


def slot_kernel(nonzero, rows_gate, rows_up, where, x_ref, hid_ref, wg_ref, wu_ref, cot_ref, keep_ref, give_ref, acc_ref):
    step = pl.program_id(0)
    slot = where[1] + step

    @pl.when(step == 0)
    def _():
        acc_ref[...] = jnp.zeros_like(acc_ref)

    block = wg_ref.shape[-1]
    tokens = x_ref.shape[2]
    per = x_ref.shape[3] // block
    depth = nonzero * block
    rep = where[0]

    def product(rows, w_ref):
        parts = []
        for k in range(nonzero):
            row = rows[slot, k]
            owner = lax.div(row, per)
            lanes = pl.ds(pl.multiple_of((row - owner * per) * block, block), block)
            parts.append(x_ref[owner, :, :, lanes].reshape(-1, block))
        return jnp.dot(
            jnp.concatenate(parts, axis=1), w_ref[0].reshape(depth, block),
            preferred_element_type=jnp.float32,
        )

    gate = product(rows_gate, wg_ref)
    up = product(rows_up, wu_ref)
    hid = hid_ref[:, 0].reshape(-1, block).astype(jnp.float32)
    p = jax.nn.sigmoid(gate)
    gate_cot = (hid * up * p * (1.0 + gate * (1.0 - p))).astype(jnp.bfloat16)
    up_cot = (hid * gate * p).astype(jnp.bfloat16)
    cot_ref[0, 0] = gate_cot
    cot_ref[0, 1] = up_cot
    core = lax.rem(rep, 2)
    pair = pl.ds(pl.multiple_of((rep - core) * tokens, 2 * tokens), 2 * tokens)
    for which, (rows, w_ref) in enumerate(((rows_gate, wg_ref), (rows_up, wu_ref))):
        cot = cot_ref[0, which, pair, :].T
        back = jnp.dot(w_ref[0].reshape(depth, block), cot, preferred_element_type=jnp.float32)
        for k in range(nonzero):
            acc_ref[rows[slot, k]] += back[k * block : (k + 1) * block]

    @pl.when(step == pl.num_programs(0) - 1)
    def _():
        own = pl.ds(pl.multiple_of(core * tokens, tokens), tokens)
        other = pl.ds(pl.multiple_of((1 - core) * tokens, tokens), tokens)
        for r in range(acc_ref.shape[0]):
            lanes = pl.ds((r % per) * block, block)
            keep_ref[r // per, :, lanes] = acc_ref[r, :, own].T
            give_ref[r // per, :, lanes] = acc_ref[r, :, other].T.astype(jnp.bfloat16)


def slots_call(rows_gate, rows_up, where, x_all, hid_all, wg, wu):
    owners, replicas, tokens, width = x_all.shape
    block = wg.shape[-1]
    slot_count, nonzero = wg.shape[0] // 2, wg.shape[1]
    row_blocks = owners * width // block
    weight = pl.BlockSpec((1, nonzero, block, block), lambda i, a, b, c: (c[1] + i, 0, 0, 0))
    grad_spec = pl.BlockSpec((owners, tokens, width), lambda i, a, b, c: (0, 0, 0))
    return pl.pallas_call(
        functools.partial(slot_kernel, nonzero),
        grid_spec=pltpu.PrefetchScalarGridSpec(
            num_scalar_prefetch=3,
            grid=(slot_count,),
            in_specs=[
                pl.BlockSpec(x_all.shape, lambda i, a, b, c: (0, 0, 0, 0)),
                pl.BlockSpec((replicas, 1, tokens, block), lambda i, a, b, c: (0, c[1] + i, 0, 0)),
                weight,
                weight,
            ],
            out_specs=[
                pl.BlockSpec((1, 2, replicas * tokens, block), lambda i, a, b, c: (i, 0, 0, 0)),
                grad_spec,
                grad_spec,
            ],
            scratch_shapes=[pltpu.VMEM((row_blocks, block, 2 * tokens), jnp.float32)],
        ),
        out_shape=[
            jax.ShapeDtypeStruct((slot_count, 2, replicas * tokens, block), jnp.bfloat16),
            jax.ShapeDtypeStruct((owners, tokens, width), jnp.float32),
            jax.ShapeDtypeStruct((owners, tokens, width), jnp.bfloat16),
        ],
        compiler_params=pltpu.CompilerParams(
            dimension_semantics=("arbitrary",), vmem_limit_bytes=VMEM_LIMIT
        ),
        cost_estimate=pl.CostEstimate(
            flops=slot_count * nonzero * 2 * 6 * 2 * tokens * block * block,
            bytes_accessed=slot_count * nonzero * 4 * block * block,
            transcendentals=0,
        ),
    )(rows_gate, rows_up, where, x_all, hid_all, wg, wu)


def grad_slot(step, where, half):
    late = step >= half
    return jnp.where(late, half - where[0] + step - half, where[0] + step)


def grad_kernel(half, rows_gate, rows_up, where, x_ref, cot_ref, sib_ref, gg_ref, gu_ref, xt_ref):
    step = pl.program_id(0)
    slot = grad_slot(step, where, half)
    own, block = gg_ref.shape[1], gg_ref.shape[-1]

    @pl.when(step == 0)
    def _():
        per = x_ref.shape[3] // block
        for r in range(xt_ref.shape[0]):
            lanes = pl.ds((r % per) * block, block)
            xt_ref[r] = x_ref[r // per, :, :, lanes].reshape(-1, block).T

    def work(source):
        for which, (rows, out_ref) in enumerate(((rows_gate, gg_ref), (rows_up, gu_ref))):
            lhs = jnp.concatenate([xt_ref[rows[slot, k]] for k in range(own)], axis=0)
            both = jnp.dot(lhs, source[0, which], preferred_element_type=jnp.float32)
            out_ref[0] = both.reshape(own, block, block).astype(jnp.bfloat16)

    @pl.when(step < half)
    def _():
        work(cot_ref)

    @pl.when(step >= half)
    def _():
        work(sib_ref)


def grads_call(rows_gate, rows_up, where, x_all, cots, sib_cots):
    slot_count, own = rows_gate.shape
    half, _, tokens, block = cots.shape
    row_blocks = x_all.shape[0] * x_all.shape[3] // block
    out = jax.ShapeDtypeStruct((slot_count, own, block, block), jnp.bfloat16)
    out_spec = pl.BlockSpec(
        (1, own, block, block), lambda i, a, b, c: (grad_slot(i, c, half), 0, 0, 0)
    )
    return pl.pallas_call(
        functools.partial(grad_kernel, half),
        grid_spec=pltpu.PrefetchScalarGridSpec(
            num_scalar_prefetch=3,
            grid=(slot_count,),
            in_specs=[
                pl.BlockSpec(x_all.shape, lambda i, a, b, c: (0, 0, 0, 0)),
                pl.BlockSpec(
                    (1, 2, tokens, block), lambda i, a, b, c: (jnp.minimum(i, half - 1), 0, 0, 0)
                ),
                pl.BlockSpec(
                    (1, 2, tokens, block), lambda i, a, b, c: (jnp.maximum(i - half, 0), 0, 0, 0)
                ),
            ],
            out_specs=[out_spec, out_spec],
            scratch_shapes=[pltpu.VMEM((row_blocks, block, tokens), jnp.bfloat16)],
        ),
        out_shape=[out, out],
        compiler_params=pltpu.CompilerParams(
            dimension_semantics=("arbitrary",), vmem_limit_bytes=VMEM_LIMIT
        ),
        cost_estimate=pl.CostEstimate(
            flops=slot_count * own * 2 * 2 * tokens * block * block,
            bytes_accessed=slot_count * own * 4 * block * block,
            transcendentals=0,
        ),
    )(rows_gate, rows_up, where, x_all, cots, sib_cots)


def body(tokens_in, hidden_grad, gate_blocks, up_blocks, gate_rows, up_rows, column_of_slot):
    slot_count, nonzero = gate_blocks.shape[:2]
    column_count = gate_rows.shape[0]
    replicas = lax.axis_size("dp")
    own = nonzero // replicas
    column_hot = (
        column_of_slot[:, None] == jnp.arange(column_count, dtype=jnp.int32)[None, :]
    ).astype(jnp.int32)
    rows_gate = jnp.sum(column_hot[:, :, None] * gate_rows[None, :, :], axis=1)
    rows_up = jnp.sum(column_hot[:, :, None] * up_rows[None, :, :], axis=1)
    in_use = (column_of_slot < column_count).astype(jnp.bfloat16)

    hid = (hidden_grad * in_use[None, :, None]).transpose(1, 0, 2)
    x_all, hid_all = gather_all(tokens_in, hid)

    index = lax.axis_index("dp")
    own_gate = lax.dynamic_slice_in_dim(rows_gate, index * own, own, axis=1)
    own_up = lax.dynamic_slice_in_dim(rows_up, index * own, own, axis=1)

    half = slot_count // 2
    core = lax.rem(index, 2)
    first = (core * half).reshape(1).astype(jnp.int32)
    where = jnp.stack([index.astype(jnp.int32), first[0]])
    swap = [(i, i + 1 - 2 * (i % 2)) for i in range(replicas)]
    cots, keep, give = slots_call(
        rows_gate, rows_up, where, x_all, hid_all, gate_blocks, up_blocks
    )
    got = lax.ppermute(give, "dp", swap)
    total = (keep + got.astype(jnp.float32)).astype(jnp.bfloat16)
    total, cots = lax.optimization_barrier((total, cots))
    sib_cots = lax.ppermute(cots, "dp", swap)
    arrived = lax.all_to_all(
        total, "tensor", split_axis=0, concat_axis=0, tiled=True
    )
    gate_grad, up_grad = grads_call(own_gate, own_up, first, x_all, cots, sib_cots)
    arrived, gate_grad, up_grad = lax.optimization_barrier((arrived, gate_grad, up_grad))
    tokens_grad = jnp.sum(arrived.astype(jnp.float32), axis=0).astype(jnp.bfloat16)
    return (tokens_grad, gate_grad, up_grad)


def solution(mesh):
    placed = (
        P(("groups", "dp"), "tensor"),
        P(("groups", "dp"), "tensor", None),
        P("tensor", None, None, None),
        P("tensor", None, None, None),
        P(),
        P(),
        P("tensor"),
    )
    return jax.shard_map(
        body,
        mesh=mesh,
        in_specs=placed,
        out_specs=(
            P(("groups", "dp"), "tensor"),
            P("tensor", ("groups", "dp"), None, None),
            P("tensor", ("groups", "dp"), None, None),
        ),
        check_vma=False,
    )
```
